512 devices in a mesh: dp: 8 (over x, core), worker: 64 (over z, y).
Axes of the slice: x: 4, y: 8, z: 8, core: 2. Of those that a mesh axis runs over, the one named last changes fastest.
Arguments:
- partials: bfloat16 [8, 192, 512, 512], P('dp', None, 'worker'), may hold values from -6 to 6
- stats: float32 [8, 64, 2, 512, 512], P('dp', 'worker'), as said below
- roots: bfloat16 [8, 64, 2, 512, 512], P('dp', 'worker'), as said below
- owner: int32 [192], replicated, may hold values from 0 to 63, as said below
- refresh: int32 [64], replicated, may hold values from 0 to 191, as said below
Outputs:
- directions: bfloat16 [192, 512, 512], P('dp', 'worker')
The draws below stay inside these ranges and needn't reach their ends.
Inputs may be any that keep to these rules, and one draw needn't show every extreme that they name: `owner`: within the 24 blocks of one group, blocks r * 24 to r * 24 + 23, the owners are distinct workers. `refresh`: 64 distinct block indices. `stats`: each matrix is symmetric positive definite. `roots`: each matrix is symmetric positive definite.
All inputs are finite; a program needn't handle non-finite values.
Results may differ from the reference program's by a relative error of at most 0.02.
Values may be sent and summed in bfloat16 or wider, within the bound.
A program may use at most 64 MiB of HBM per device.

```python
import jax
import jax.numpy as jnp
from jax import lax

O = 512
ITERS = 3
ROWS = 8
WORKERS = 64
RB = 24
NBLK = 192
NREF = 64


def symmetric_definite(noise_key, row_scale, block_order, lead_shape):
    noise = jax.random.uniform(noise_key, lead_shape + (block_order, block_order), jnp.float32, -1.0, 1.0)
    sym_part = 0.5 * (noise + jnp.swapaxes(noise, -1, -2))
    eye_part = jnp.eye(block_order, dtype=jnp.float32) * (1.7 * block_order ** 0.5)
    root_scale = jnp.sqrt(row_scale)
    return root_scale[..., :, None] * (eye_part + sym_part) * root_scale[..., None, :]


def draw_stats(key, part):
    key = jax.random.fold_in(key, 11)
    scale_key, noise_key = jax.random.split(key)
    lead_shape = (ROWS, WORKERS, 2)
    row_scale = jax.random.uniform(scale_key, lead_shape + (O,), jnp.float32, 0.6, 1.5)
    return symmetric_definite(noise_key, row_scale, O, lead_shape) * O ** 0.5


def draw_roots(key, part):
    key = jax.random.fold_in(key, 12)
    scale_key, noise_key = jax.random.split(key)
    lead_shape = (ROWS, WORKERS, 2)
    row_scale = jax.random.uniform(scale_key, lead_shape + (O,), jnp.float32, 0.5, 1.5)
    return (symmetric_definite(noise_key, row_scale, O, lead_shape) / (1.7 * O ** 0.5)).astype(jnp.bfloat16)


def draw_owner(key, part):
    key = jax.random.fold_in(key, 13)
    row_keys = jax.random.split(key, ROWS)
    shuffled = jax.vmap(lambda row_key: jax.random.permutation(row_key, WORKERS))(row_keys)
    return shuffled[:, :RB].reshape(ROWS * RB).astype(jnp.int32)


def draw_refresh(key, part):
    key = jax.random.fold_in(key, 14)
    return jax.random.permutation(key, NBLK)[:NREF].astype(jnp.int32)


def shard_levels(stream_key, dims, pieces, least, high):
    factor_of = 1.0
    for position, shards_of in pieces:
        draws = jax.random.uniform(jax.random.fold_in(jax.random.fold_in(stream_key, 6), position), (shards_of,), jnp.float32, least / len(pieces), high / len(pieces))
        factor_of = factor_of * jnp.repeat(jnp.exp(draws), dims[position] // shards_of).reshape((-1,) + (1,) * (len(dims) - 1 - position))
    return factor_of


def centred(own_key, dims, spread, reach, cuts=(), held_as=jnp.bfloat16):
    result = jax.random.normal(own_key, dims, jnp.float32) * spread
    if len(cuts) > 0:
        result = shard_levels(own_key, dims, cuts, -0.22, 0.18) * result
    return jnp.clip(result, min=-reach, max=reach).astype(held_as)


def setup_inputs(seed: int = 0) -> dict:
    key_list = jax.random.split(jax.random.key(seed), 6)
    partials = centred(key_list[0], (ROWS, NBLK, O, O), 1.0, 6.0, ((0, 8), (2, 64)))
    stats = draw_stats(jax.random.fold_in(key_list[5], 71), 0)
    roots = draw_roots(jax.random.fold_in(key_list[5], 71), 0)
    owner = draw_owner(jax.random.fold_in(key_list[5], 71), 0)
    refresh = draw_refresh(jax.random.fold_in(key_list[5], 71), 0)
    return dict(partials=partials, stats=stats, roots=roots, owner=owner, refresh=refresh)


STAT_DECAY = 0.9
EPSILON = 1e-06

def matmul(left_operand, right_operand):
    return jnp.dot(left_operand, right_operand, preferred_element_type=jnp.float32)

def normalize(stat_matrix):
    frob_scale = jnp.sqrt(jnp.sum(stat_matrix * stat_matrix) + EPSILON)
    return (stat_matrix / frob_scale).astype(jnp.bfloat16)

def newton(current):
    block_order = current.shape[0]
    identity = jnp.eye(block_order, dtype=jnp.float32)
    root_iter = current
    for iteration in range(ITERS):
        factor = ((5.0 * identity - current.astype(jnp.float32)) * 0.25).astype(jnp.bfloat16)
        if iteration == 0:
            root_iter = factor
        else:
            root_iter = matmul(root_iter, factor).astype(jnp.bfloat16)
        if iteration + 1 < ITERS:
            square = matmul(factor, factor).astype(jnp.bfloat16)
            partial_prod = matmul(square, current).astype(jnp.bfloat16)
            current = matmul(partial_prod, square).astype(jnp.bfloat16)
    return root_iter

def one_block(block_id, partials, stats, roots, owner, refresh):
    group_row = (block_id // RB).astype(jnp.int32)
    worker_id = owner[block_id].astype(jnp.int32)
    gradient = lax.optimization_barrier(jnp.sum(partials[:, block_id].astype(jnp.float32), axis=0)).astype(jnp.bfloat16)
    stat_pair = stats[group_row, worker_id]
    old_pair = roots[group_row, worker_id]
    listed = jnp.any(refresh == block_id)

    def refresh_both():
        left_stat = STAT_DECAY * stat_pair[0] + (1.0 - STAT_DECAY) * matmul(gradient, gradient.T)
        right_stat = STAT_DECAY * stat_pair[1] + (1.0 - STAT_DECAY) * matmul(gradient.T, gradient)
        return (newton(normalize(left_stat)), newton(normalize(right_stat)))

    def keep_old():
        return (old_pair[0], old_pair[1])
    left_root, right_root = lax.cond(listed, refresh_both, keep_old)
    left_side = matmul(left_root, gradient).astype(jnp.bfloat16)
    raw_dir = matmul(left_side, right_root)
    grad_norm = jnp.sqrt(jnp.sum(jnp.square(gradient.astype(jnp.float32))))
    dir_norm = jnp.sqrt(jnp.sum(raw_dir * raw_dir) + EPSILON)
    return (raw_dir * (grad_norm / dir_norm)).astype(jnp.bfloat16)

def reference(partials, stats, roots, owner, refresh):
    block_ids = jnp.arange(NBLK, dtype=jnp.int32)
    return lax.map(lambda block_id: one_block(block_id, partials, stats, roots, owner, refresh), block_ids)
```

```python
import functools

import jax
import jax.numpy as jnp
from jax import lax
from jax.experimental import pallas as pl
from jax.experimental.pallas import tpu as pltpu
from jax.sharding import PartitionSpec as P

ITERS = 3
STAT_DECAY = 0.9
EPSILON = 1e-06
MESH = pl.DeviceIdType.MESH
CHUNKS = ((0, 256), (256, 256))
NB = 256


def dot(a, b):
    return jnp.dot(a, b, preferred_element_type=jnp.float32)


def dot_nt(a, b):
    return lax.dot_general(a, b, (((1,), (1,)), ((), ())), preferred_element_type=jnp.float32)


def row_blocks(order):
    return [pl.ds(i, NB) for i in range(0, order, NB)]


def product(a_ref, b_ref, c_ref):
    for rows in row_blocks(a_ref.shape[0]):
        c_ref[rows, :] = dot(a_ref[rows, :], b_ref[...]).astype(c_ref.dtype)


def factor_of(m_ref, f_ref):
    order = m_ref.shape[0]
    for i in range(0, order, NB):
        rows = pl.ds(i, NB)
        row = lax.broadcasted_iota(jnp.int32, (NB, order), 0) + i
        col = lax.broadcasted_iota(jnp.int32, (NB, order), 1)
        five = jnp.where(row == col, 5.0, 0.0)
        f_ref[rows, :] = ((five - m_ref[rows, :].astype(jnp.float32)) * 0.25).astype(jnp.bfloat16)


def normalized(stat_ref, side, grams, m_ref):
    total = jnp.zeros((), jnp.float32)
    order = m_ref.shape[0]
    for rows in row_blocks(order):
        mixed = STAT_DECAY * stat_ref[side, rows, :] + (1.0 - STAT_DECAY) * grams(rows)
        stat_ref[side, rows, :] = mixed
        total = total + jnp.sum(mixed * mixed)
    scale = lax.rsqrt(jnp.full((1, order), total + EPSILON, jnp.float32))
    for rows in row_blocks(order):
        m_ref[rows, :] = (stat_ref[side, rows, :] * scale).astype(jnp.bfloat16)


def newton_pair(m, f, x, q, t):
    for it in range(ITERS):
        for s in range(2):
            factor_of(m[s], f[s])
        if it == 0:
            for s in range(2):
                x[s][...] = f[s][...]
        else:
            for s in range(2):
                product(x[s], f[s], t[s])
            for s in range(2):
                x[s][...] = t[s][...]
        if it + 1 < ITERS:
            for s in range(2):
                product(f[s], f[s], q[s])
            for s in range(2):
                product(q[s], m[s], t[s])
            for s in range(2):
                product(t[s], q[s], m[s])


def compute(fresh, g_ref, gt_ref, stat_ref, root_ref, m, f, x, q, t, raw_ref, dir_ref):
    order = g_ref.shape[0]
    normalized(stat_ref, 0, lambda rows: dot(g_ref[rows, :], gt_ref[...]), m[0])
    normalized(stat_ref, 1, lambda rows: dot(gt_ref[rows, :], g_ref[...]), m[1])
    newton_pair(m, f, x, q, t)
    take = jnp.full((1, order), fresh, jnp.int32) > 0
    for s in range(2):
        for rows in row_blocks(order):
            x[s][rows, :] = jnp.where(
                take, x[s][rows, :].astype(jnp.float32), root_ref[s, rows, :].astype(jnp.float32)
            ).astype(jnp.bfloat16)
    product(x[0], g_ref, t[0])
    grad_sq = jnp.zeros((), jnp.float32)
    raw_sq = jnp.zeros((), jnp.float32)
    for rows in row_blocks(order):
        raw = dot(t[0][rows, :], x[1][...])
        raw_ref[rows, :] = raw
        raw_sq = raw_sq + jnp.sum(raw * raw)
        g32 = g_ref[rows, :].astype(jnp.float32)
        grad_sq = grad_sq + jnp.sum(g32 * g32)
    scale = jnp.sqrt(jnp.full((1, order), grad_sq, jnp.float32)) / jnp.sqrt(
        jnp.full((1, order), raw_sq + EPSILON, jnp.float32)
    )
    for i in range(0, order, NB):
        d = (raw_ref[pl.ds(i, NB), :] * scale).reshape(NB // 8, 8, order)
        dir_ref[pl.ds(i // 8, NB // 8)] = d.astype(jnp.bfloat16)


def kernel(
    part_ref, stats_hbm, roots_hbm, owner_ref, refresh_ref, out_ref,
    own, pair, recvx, summed, outgoing, gath, ret, dirs, slot_ref,
    g_ref, gt_ref, stat_ref, root_ref, m0, m1, f0, f1, x0, x1, q0, q1, t0, t1, raw_ref,
    load_sem, own_sem, pair_send, pair_recv, x_send, x_recv, a_send, a_recv, r_send, r_recv,
):
    chips, blocks, rows8, order = own.shape
    workers = gath.shape[0]
    g, w = lax.axis_index("dp"), lax.axis_index("worker")
    x, c = lax.div(g, 2), lax.rem(g, 2)
    nc = len(CHUNKS)

    def other_worker(i):
        return lax.rem(w + i, workers)

    barrier = pltpu.get_barrier_semaphore()
    pl.semaphore_signal(barrier, inc=1, device_id=(x * 2 + 1 - c, w), device_id_type=MESH)
    for i in range(1, chips):
        to = lax.rem(x + i, chips) * 2 + c
        pl.semaphore_signal(barrier, inc=1, device_id=(to, w), device_id_type=MESH)

    def greet(i, carry):
        pl.semaphore_signal(barrier, inc=1, device_id=(g, other_worker(i)), device_id_type=MESH)
        return carry

    lax.fori_loop(1, workers, greet, 0)

    def own_copy(j, t):
        cols = pl.ds(*CHUNKS[j])
        return pltpu.make_async_copy(
            part_ref.at[t, c, :, :, cols], own.at[t, :, :, cols], own_sem.at[j, t]
        )

    def pair_copy(j, t):
        cols = pl.ds(*CHUNKS[j])
        return pltpu.make_async_remote_copy(
            part_ref.at[t, 1 - c, :, :, cols], pair.at[t, :, :, cols],
            pair_send.at[j, t], pair_recv.at[j, t],
            device_id=(x * 2 + 1 - c, w), device_id_type=MESH,
        )

    def x_copy(j, i):
        cols = pl.ds(*CHUNKS[j])
        to = lax.rem(x + i, chips)
        return pltpu.make_async_remote_copy(
            own.at[to, :, :, cols], recvx.at[i - 1, :, :, cols],
            x_send.at[j, i - 1], x_recv.at[j, i - 1],
            device_id=(to * 2 + c, w), device_id_type=MESH,
        )

    def a_copy(j, to):
        cols = pl.ds(*CHUNKS[j])
        return pltpu.make_async_remote_copy(
            outgoing.at[to, :, cols], gath.at[w, :, cols], a_send.at[j], a_recv.at[j],
            device_id=(g, to), device_id_type=MESH,
        )

    def a_all(j):
        cols, rest = pl.ds(*CHUNKS[j]), pl.ds(0, workers - 1)
        return pltpu.make_async_remote_copy(
            outgoing.at[rest, :, cols], gath.at[rest, :, cols], a_send.at[j], a_recv.at[j],
            device_id=(g, w), device_id_type=MESH,
        )

    def r_copy(to):
        return pltpu.make_async_remote_copy(
            dirs.at[to], ret.at[w], r_send, r_recv, device_id=(g, to), device_id_type=MESH
        )

    def r_all():
        rest = pl.ds(0, workers - 1)
        return pltpu.make_async_remote_copy(
            dirs.at[rest], ret.at[rest], r_send, r_recv, device_id=(g, w), device_id_type=MESH
        )

    hops = (2, 1, 3, 0)
    for j in range(nc):
        for i in hops:
            own_copy(j, lax.rem(x + i, chips)).start()
    stat_load = pltpu.make_async_copy(stats_hbm, stat_ref, load_sem.at[0])
    root_load = pltpu.make_async_copy(roots_hbm, root_ref, load_sem.at[1])
    stat_load.start()
    root_load.start()
    pl.semaphore_wait(barrier, chips + workers - 1)
    for j in range(nc):
        for i in hops:
            pair_copy(j, lax.rem(x + i, chips)).start()

    step = 8
    for j in range(nc):
        cols = pl.ds(*CHUNKS[j])
        for i in hops:
            t = lax.rem(x + i, chips)
            own_copy(j, t).wait()
            pair_copy(j, t).wait_recv()
            if i == 0:
                continue
            for k in range(0, blocks, step):
                ks = pl.ds(k, step)
                own[t, ks, :, cols] = (
                    own[t, ks, :, cols].astype(jnp.float32) + pair[t, ks, :, cols].astype(jnp.float32)
                ).astype(jnp.bfloat16)
            x_copy(j, i).start()

    first = g * blocks

    def find_slot(t, carry):
        slot = jnp.int32(0)
        for k in range(blocks):
            slot = jnp.where(owner_ref[first + k] == t, k, slot)
        slot_ref[t] = slot
        return carry

    lax.fori_loop(0, workers, find_slot, 0)

    for j in range(nc):
        cols = pl.ds(*CHUNKS[j])
        for i in range(1, chips):
            x_copy(j, i).wait_recv()
        for k in range(0, blocks, step):
            ks = pl.ds(k, step)
            total = own[x, ks, :, cols].astype(jnp.float32) + pair[x, ks, :, cols].astype(jnp.float32)
            for i in range(chips - 1):
                total = total + recvx[i, ks, :, cols].astype(jnp.float32)
            summed[ks, :, cols] = total.astype(jnp.bfloat16)

        def pack(i, carry):
            to = other_worker(i)
            outgoing[to, :, cols] = summed[slot_ref[to], :, cols]
            a_copy(j, to).start()
            return carry

        lax.fori_loop(1, workers, pack, 0)
        gath[w, :, cols] = summed[slot_ref[w], :, cols]

    mine = first + slot_ref[w]

    def is_listed(i, carry):
        return carry + jnp.where(refresh_ref[i] == mine, 1, 0)

    fresh = lax.fori_loop(0, refresh_ref.shape[0], is_listed, jnp.int32(0))

    for j in range(nc):
        cols = pl.ds(*CHUNKS[j])
        a_all(j).wait_recv()
        for i in range(0, workers, 16):
            piece = gath[pl.ds(i, 16), :, cols].astype(jnp.float32).reshape(16 * rows8, CHUNKS[j][1])
            g_ref[pl.ds(i * rows8, 16 * rows8), cols] = piece.astype(jnp.bfloat16)
        gt_ref[cols, :] = g_ref[:, cols].T
    stat_load.wait()
    root_load.wait()
    compute(
        fresh, g_ref, gt_ref, stat_ref, root_ref, (m0, m1), (f0, f1), (x0, x1), (q0, q1), (t0, t1),
        raw_ref, dirs,
    )

    def send_back(i, carry):
        r_copy(other_worker(i)).start()
        return carry

    lax.fori_loop(1, workers, send_back, 0)
    ret[w] = dirs[w]
    for j in range(nc):
        for i in range(chips):
            pair_copy(j, i).wait_send()
        for i in range(1, chips):
            x_copy(j, i).wait_send()
        a_all(j).wait_send()
    r_all().wait_recv()
    for k in range(blocks):
        out_ref[k] = ret[owner_ref[first + k]]
    r_all().wait_send()


def on_device(partials, stats, roots, owner, refresh):
    workers, replicas = lax.axis_size("worker"), lax.axis_size("dp")
    _, total, rows, order = partials.shape
    chips, blocks = replicas // 2, total // replicas
    nc = len(CHUNKS)
    bf, dma = functools.partial(pltpu.VMEM, dtype=jnp.bfloat16), pltpu.SemaphoreType.DMA
    square = bf((order, order))
    return pl.pallas_call(
        kernel,
        out_shape=jax.ShapeDtypeStruct((blocks, rows, order), jnp.bfloat16),
        in_specs=[pl.BlockSpec(memory_space=pl.ANY)] * 3
        + [pl.BlockSpec(memory_space=pltpu.SMEM)] * 2,
        out_specs=pl.BlockSpec(memory_space=pltpu.VMEM),
        scratch_shapes=[
            bf((chips, blocks, rows, order)),
            bf((chips, blocks, rows, order)),
            bf((chips - 1, blocks, rows, order)),
            bf((blocks, rows, order)),
            bf((workers, rows, order)),
            bf((workers, rows, order)),
            bf((workers, rows, order)),
            bf((workers, rows, order)),
            pltpu.SMEM((workers,), jnp.int32),
            square,
            square,
            pltpu.VMEM((2, order, order), jnp.float32),
            bf((2, order, order)),
        ]
        + [square] * 10
        + [
            pltpu.VMEM((order, order), jnp.float32),
            dma((2,)),
            dma((nc, chips)),
            dma((nc, chips)),
            dma((nc, chips)),
            dma((nc, chips - 1)),
            dma((nc, chips - 1)),
            dma((nc,)),
            dma((nc,)),
            dma,
            dma,
        ],
        compiler_params=pltpu.CompilerParams(
            collective_id=0, has_side_effects=True, vmem_limit_bytes=56 * 2**20
        ),
    )(
        partials.reshape(chips, 2, blocks, rows, order),
        stats.reshape(2, order, order),
        roots.reshape(2, order, order),
        owner,
        refresh,
    )


def solution(mesh):
    in_specs = (
        P("dp", None, "worker", None),
        P("dp", "worker", None, None, None),
        P("dp", "worker", None, None, None),
        P(),
        P(),
    )
    return jax.shard_map(
        on_device,
        mesh=mesh,
        in_specs=in_specs,
        out_specs=P("dp", "worker", None),
        check_vma=False,
    )
```

```python
import functools

import jax
import jax.numpy as jnp
from jax import lax
from jax.experimental import pallas as pl
from jax.experimental.pallas import tpu as pltpu
from jax.sharding import PartitionSpec as P

ITERS = 3
STAT_DECAY = 0.9
EPSILON = 1e-06
MESH = pl.DeviceIdType.MESH
SIDE = 8
CHUNKS = ((0, 128), (128, 128), (256, 256))
NB = 256


def dot(a, b):
    return jnp.dot(a, b, preferred_element_type=jnp.float32)


def dot_nt(a, b):
    return lax.dot_general(a, b, (((1,), (1,)), ((), ())), preferred_element_type=jnp.float32)


def row_blocks(order):
    return [pl.ds(i, NB) for i in range(0, order, NB)]


def product(a_ref, b_ref, c_ref):
    for rows in row_blocks(a_ref.shape[0]):
        c_ref[rows, :] = dot(a_ref[rows, :], b_ref[...]).astype(c_ref.dtype)


def factor_of(m_ref, f_ref):
    order = m_ref.shape[0]
    for i in range(0, order, NB):
        rows = pl.ds(i, NB)
        row = lax.broadcasted_iota(jnp.int32, (NB, order), 0) + i
        col = lax.broadcasted_iota(jnp.int32, (NB, order), 1)
        five = jnp.where(row == col, 5.0, 0.0)
        f_ref[rows, :] = ((five - m_ref[rows, :].astype(jnp.float32)) * 0.25).astype(jnp.bfloat16)


def normalized(stat_ref, side, grams, m_ref):
    total = jnp.zeros((), jnp.float32)
    order = m_ref.shape[0]
    for rows in row_blocks(order):
        mixed = STAT_DECAY * stat_ref[side, rows, :] + (1.0 - STAT_DECAY) * grams(rows)
        stat_ref[side, rows, :] = mixed
        total = total + jnp.sum(mixed * mixed)
    scale = lax.rsqrt(jnp.full((1, order), total + EPSILON, jnp.float32))
    for rows in row_blocks(order):
        m_ref[rows, :] = (stat_ref[side, rows, :] * scale).astype(jnp.bfloat16)


def newton_pair(m, f, x, q, t):
    for it in range(ITERS):
        for s in range(2):
            factor_of(m[s], f[s])
        if it == 0:
            for s in range(2):
                x[s][...] = f[s][...]
        else:
            for s in range(2):
                product(x[s], f[s], t[s])
            for s in range(2):
                x[s][...] = t[s][...]
        if it + 1 < ITERS:
            for s in range(2):
                product(f[s], f[s], q[s])
            for s in range(2):
                product(q[s], m[s], t[s])
            for s in range(2):
                product(t[s], q[s], m[s])


def compute(fresh, g_ref, gt_ref, stat_ref, root_ref, m, f, x, q, t, raw_ref, dir_ref):
    order = g_ref.shape[0]
    normalized(stat_ref, 0, lambda rows: dot(g_ref[rows, :], gt_ref[...]), m[0])
    normalized(stat_ref, 1, lambda rows: dot(gt_ref[rows, :], g_ref[...]), m[1])
    newton_pair(m, f, x, q, t)
    take = jnp.full((1, order), fresh, jnp.int32) > 0
    for s in range(2):
        for rows in row_blocks(order):
            x[s][rows, :] = jnp.where(
                take, x[s][rows, :].astype(jnp.float32), root_ref[s, rows, :].astype(jnp.float32)
            ).astype(jnp.bfloat16)
    product(x[0], g_ref, t[0])
    grad_sq = jnp.zeros((), jnp.float32)
    raw_sq = jnp.zeros((), jnp.float32)
    for rows in row_blocks(order):
        raw = dot(t[0][rows, :], x[1][...])
        raw_ref[rows, :] = raw
        raw_sq = raw_sq + jnp.sum(raw * raw)
        g32 = g_ref[rows, :].astype(jnp.float32)
        grad_sq = grad_sq + jnp.sum(g32 * g32)
    scale = jnp.sqrt(jnp.full((1, order), grad_sq, jnp.float32)) / jnp.sqrt(
        jnp.full((1, order), raw_sq + EPSILON, jnp.float32)
    )
    for i in range(0, order, NB):
        d = (raw_ref[pl.ds(i, NB), :] * scale).reshape(NB // 8, 8, order)
        dir_ref[pl.ds(i // 8, NB // 8)] = d.astype(jnp.bfloat16)


def kernel(
    part_ref, stats_hbm, roots_hbm, owner_ref, refresh_ref, out_ref,
    own, pair, recvx, summed, outgoing, gath, ret, dirs, slot_ref,
    g_ref, gt_ref, stat_ref, root_ref, m0, m1, f0, f1, x0, x1, q0, q1, t0, t1, raw_ref,
    load_sem, own_sem, pair_send, pair_recv, x_send, x_recv, a_send, a_recv, r_send, r_recv, line_sem,
):
    chips, blocks, rows8, order = own.shape
    workers = gath.shape[0]
    g, w = lax.axis_index("dp"), lax.axis_index("worker")
    x, c = lax.div(g, 2), lax.rem(g, 2)
    nc = len(CHUNKS)

    def other_worker(i):
        return lax.rem(w + i, workers)

    barrier = pltpu.get_barrier_semaphore()
    pl.semaphore_signal(barrier, inc=1, device_id=(x * 2 + 1 - c, w), device_id_type=MESH)
    for i in range(1, chips):
        to = lax.rem(x + i, chips) * 2 + c
        pl.semaphore_signal(barrier, inc=1, device_id=(to, w), device_id_type=MESH)

    side = SIDE
    z, y = lax.div(w, side), lax.rem(w, side)
    for i in range(1, side):
        beside = z * side + lax.rem(y + i, side)
        above = lax.rem(z + i, side) * side + y
        pl.semaphore_signal(barrier, inc=1, device_id=(g, beside), device_id_type=MESH)
        pl.semaphore_signal(barrier, inc=1, device_id=(g, above), device_id_type=MESH)

    def own_copy(j, t):
        cols = pl.ds(*CHUNKS[j])
        return pltpu.make_async_copy(
            part_ref.at[t, c, :, :, cols], own.at[t, :, :, cols], own_sem.at[j, t]
        )

    def pair_copy(j, t):
        cols = pl.ds(*CHUNKS[j])
        return pltpu.make_async_remote_copy(
            part_ref.at[t, 1 - c, :, :, cols], pair.at[t, :, :, cols],
            pair_send.at[j, t], pair_recv.at[j, t],
            device_id=(x * 2 + 1 - c, w), device_id_type=MESH,
        )

    def x_copy(j, i):
        cols = pl.ds(*CHUNKS[j])
        to = lax.rem(x + i, chips)
        return pltpu.make_async_remote_copy(
            own.at[to, :, :, cols], recvx.at[i - 1, :, :, cols],
            x_send.at[j, i - 1], x_recv.at[j, i - 1],
            device_id=(to * 2 + c, w), device_id_type=MESH,
        )

    def a_copy(j, to):
        cols = pl.ds(*CHUNKS[j])
        return pltpu.make_async_remote_copy(
            outgoing.at[to, :, cols], gath.at[w, :, cols], a_send.at[j], a_recv.at[j],
            device_id=(g, to), device_id_type=MESH,
        )

    def a_all(j):
        cols, rest = pl.ds(*CHUNKS[j]), pl.ds(0, workers - 1)
        return pltpu.make_async_remote_copy(
            outgoing.at[rest, :, cols], gath.at[rest, :, cols], a_send.at[j], a_recv.at[j],
            device_id=(g, w), device_id_type=MESH,
        )

    def r_copy(to):
        return pltpu.make_async_remote_copy(
            dirs.at[to], ret.at[w], r_send, r_recv, device_id=(g, to), device_id_type=MESH
        )

    def r_all():
        rest = pl.ds(0, workers - 1)
        return pltpu.make_async_remote_copy(
            dirs.at[rest], ret.at[rest], r_send, r_recv, device_id=(g, w), device_id_type=MESH
        )

    hops = (2, 1, 3, 0)
    for j in range(nc):
        for i in hops:
            own_copy(j, lax.rem(x + i, chips)).start()
    stat_load = pltpu.make_async_copy(stats_hbm, stat_ref, load_sem.at[0])
    root_load = pltpu.make_async_copy(roots_hbm, root_ref, load_sem.at[1])
    stat_load.start()
    root_load.start()
    pl.semaphore_wait(barrier, chips + 2 * (side - 1))
    for j in range(nc):
        for i in hops:
            pair_copy(j, lax.rem(x + i, chips)).start()
    for i in range(1, side):
        above = lax.rem(z + i, side) * side + y
        pl.semaphore_signal(line_sem, inc=1, device_id=(g, above), device_id_type=MESH)

    step = 8
    for j in range(nc):
        cols = pl.ds(*CHUNKS[j])
        for i in hops:
            t = lax.rem(x + i, chips)
            own_copy(j, t).wait()
            pair_copy(j, t).wait_recv()
            if i == 0:
                continue
            for k in range(0, blocks, step):
                ks = pl.ds(k, step)
                own[t, ks, :, cols] = (
                    own[t, ks, :, cols].astype(jnp.float32) + pair[t, ks, :, cols].astype(jnp.float32)
                ).astype(jnp.bfloat16)
            x_copy(j, i).start()

    first = g * blocks

    def find_slot(t, carry):
        slot = jnp.int32(0)
        for k in range(blocks):
            slot = jnp.where(owner_ref[first + k] == t, k, slot)
        slot_ref[t] = slot
        return carry

    lax.fori_loop(0, workers, find_slot, 0)
    pl.semaphore_wait(line_sem, side - 1)

    for j in range(nc):
        cols = pl.ds(*CHUNKS[j])
        for i in range(1, chips):
            x_copy(j, i).wait_recv()
        for k in range(0, blocks, step):
            ks = pl.ds(k, step)
            total = own[x, ks, :, cols].astype(jnp.float32) + pair[x, ks, :, cols].astype(jnp.float32)
            for i in range(chips - 1):
                total = total + recvx[i, ks, :, cols].astype(jnp.float32)
            summed[ks, :, cols] = total.astype(jnp.bfloat16)

        def pack(i, carry):
            to = other_worker(i)
            outgoing[to, :, cols] = summed[slot_ref[to], :, cols]
            a_copy(j, to).start()
            return carry

        lax.fori_loop(1, workers, pack, 0)
        gath[w, :, cols] = summed[slot_ref[w], :, cols]

    mine = first + slot_ref[w]

    def is_listed(i, carry):
        return carry + jnp.where(refresh_ref[i] == mine, 1, 0)

    fresh = lax.fori_loop(0, refresh_ref.shape[0], is_listed, jnp.int32(0))

    for j in range(nc):
        cols = pl.ds(*CHUNKS[j])
        a_all(j).wait_recv()
        for i in range(0, workers, 16):
            piece = gath[pl.ds(i, 16), :, cols].astype(jnp.float32).reshape(16 * rows8, CHUNKS[j][1])
            g_ref[pl.ds(i * rows8, 16 * rows8), cols] = piece.astype(jnp.bfloat16)
        gt_ref[cols, :] = g_ref[:, cols].T
    stat_load.wait()
    root_load.wait()
    compute(
        fresh, g_ref, gt_ref, stat_ref, root_ref, (m0, m1), (f0, f1), (x0, x1), (q0, q1), (t0, t1),
        raw_ref, dirs,
    )

    turn = 1 - 2 * lax.rem(z + y, 2)

    def send_back(i, carry):
        r_copy(lax.rem(w + turn * i + workers, workers)).start()
        return carry

    lax.fori_loop(1, workers, send_back, 0)
    ret[w] = dirs[w]
    for j in range(nc):
        for i in range(chips):
            pair_copy(j, i).wait_send()
        for i in range(1, chips):
            x_copy(j, i).wait_send()
        a_all(j).wait_send()
    r_all().wait_recv()
    for k in range(blocks):
        out_ref[k] = ret[owner_ref[first + k]]
    r_all().wait_send()


def on_device(partials, stats, roots, owner, refresh):
    workers, replicas = lax.axis_size("worker"), lax.axis_size("dp")
    _, total, rows, order = partials.shape
    chips, blocks = replicas // 2, total // replicas
    nc = len(CHUNKS)
    bf, dma = functools.partial(pltpu.VMEM, dtype=jnp.bfloat16), pltpu.SemaphoreType.DMA
    square = bf((order, order))
    return pl.pallas_call(
        kernel,
        out_shape=jax.ShapeDtypeStruct((blocks, rows, order), jnp.bfloat16),
        in_specs=[pl.BlockSpec(memory_space=pl.ANY)] * 3
        + [pl.BlockSpec(memory_space=pltpu.SMEM)] * 2,
        out_specs=pl.BlockSpec(memory_space=pltpu.VMEM),
        scratch_shapes=[
            bf((chips, blocks, rows, order)),
            bf((chips, blocks, rows, order)),
            bf((chips - 1, blocks, rows, order)),
            bf((blocks, rows, order)),
            bf((workers, rows, order)),
            bf((workers, rows, order)),
            bf((workers, rows, order)),
            bf((workers, rows, order)),
            pltpu.SMEM((workers,), jnp.int32),
            square,
            square,
            pltpu.VMEM((2, order, order), jnp.float32),
            bf((2, order, order)),
        ]
        + [square] * 10
        + [
            pltpu.VMEM((order, order), jnp.float32),
            dma((2,)),
            dma((nc, chips)),
            dma((nc, chips)),
            dma((nc, chips)),
            dma((nc, chips - 1)),
            dma((nc, chips - 1)),
            dma((nc,)),
            dma((nc,)),
            dma,
            dma,
            pltpu.SemaphoreType.REGULAR,
        ],
        compiler_params=pltpu.CompilerParams(
            collective_id=0, has_side_effects=True, vmem_limit_bytes=56 * 2**20
        ),
    )(
        partials.reshape(chips, 2, blocks, rows, order),
        stats.reshape(2, order, order),
        roots.reshape(2, order, order),
        owner,
        refresh,
    )


def solution(mesh):
    in_specs = (
        P("dp", None, "worker", None),
        P("dp", "worker", None, None, None),
        P("dp", "worker", None, None, None),
        P(),
        P(),
    )
    return jax.shard_map(
        on_device,
        mesh=mesh,
        in_specs=in_specs,
        out_specs=P("dp", "worker", None),
        check_vma=False,
    )
```

```python
import functools

import jax
import jax.numpy as jnp
from jax import lax
from jax.experimental import pallas as pl
from jax.experimental.pallas import tpu as pltpu
from jax.sharding import PartitionSpec as P

ITERS = 3
STAT_DECAY = 0.9
EPSILON = 1e-06
MESH = pl.DeviceIdType.MESH
SIDE = 8
BACK = ((0, 0), (0, 1), (1, 0), (0, 2), (0, 3), (1, 1), (1, 2), (1, 3))
CHUNKS = ((0, 128), (128, 128), (256, 256))
NB = 512


def dot(a, b):
    return jnp.dot(a, b, preferred_element_type=jnp.float32)


def dot_nt(a, b):
    return lax.dot_general(a, b, (((1,), (1,)), ((), ())), preferred_element_type=jnp.float32)


def row_blocks(order):
    return [pl.ds(i, NB) for i in range(0, order, NB)]


def product(a_ref, b_ref, c_ref):
    for rows in row_blocks(a_ref.shape[0]):
        c_ref[rows, :] = dot(a_ref[rows, :], b_ref[...]).astype(c_ref.dtype)


def put(rows, m32, m_ref, f_ref):
    shape = m32.shape
    m = m32.astype(jnp.bfloat16)
    row = lax.broadcasted_iota(jnp.int32, shape, 0) + rows.start
    col = lax.broadcasted_iota(jnp.int32, shape, 1)
    five = jnp.where(row == col, 5.0, 0.0)
    m_ref[rows, :] = m
    f_ref[rows, :] = ((five - m.astype(jnp.float32)) * 0.25).astype(jnp.bfloat16)


def normalized(stat_ref, side, left, right, m_ref, f_ref):
    order = m_ref.shape[0]
    total = jnp.zeros((1, order), jnp.float32)
    for rows in row_blocks(order):
        mixed = STAT_DECAY * stat_ref[side, rows, :] + (1.0 - STAT_DECAY) * dot(left[rows, :], right[...])
        stat_ref[side, rows, :] = mixed
        total = total + jnp.sum(mixed * mixed, axis=0, keepdims=True)
    scale = lax.rsqrt(jnp.full((1, order), jnp.sum(total) + EPSILON, jnp.float32))
    for rows in row_blocks(order):
        put(rows, stat_ref[side, rows, :] * scale, m_ref, f_ref)


def compute(take, g_ref, gt_ref, stat_ref, root_ref, m, f, x, q, t, raw_ref, dir_ref):
    order = g_ref.shape[0]
    normalized(stat_ref, 0, g_ref, gt_ref, m[0], f[0])
    normalized(stat_ref, 1, gt_ref, g_ref, m[1], f[1])
    held = [f[0], f[1]]
    factor = [f[0], f[1]]
    spare = [[x[0], t[0]], [x[1], t[1]]]
    for it in range(ITERS - 1):
        if it > 0:
            for s in range(2):
                new = spare[s].pop(0)
                product(held[s], factor[s], new)
                spare[s].append(held[s])
                held[s] = new
        y = [spare[s][0] for s in range(2)]
        for s in range(2):
            product(factor[s], factor[s], q[s])
        for s in range(2):
            product(q[s], m[s], y[s])
        later = [raw_ref.at[s] for s in range(2)] if it == 0 else factor
        for s in range(2):
            for rows in row_blocks(order):
                put(rows, dot(y[s][rows, :], q[s][...]), m[s], later[s])
        factor = later
    for s in range(2):
        new = spare[s].pop(0)
        for rows in row_blocks(order):
            root = dot(held[s][rows, :], factor[s][...])
            old = root_ref[s, rows, :].astype(jnp.float32)
            new[rows, :] = jnp.where(take, root, old).astype(jnp.bfloat16)
        spare[s].append(held[s])
        held[s] = new
    product(held[0], g_ref, q[0])
    grad_sq = jnp.zeros((1, order), jnp.float32)
    raw_sq = jnp.zeros((1, order), jnp.float32)
    for rows in row_blocks(order):
        raw = dot(q[0][rows, :], held[1][...])
        stat_ref[0, rows, :] = raw
        raw_sq = raw_sq + jnp.sum(raw * raw, axis=0, keepdims=True)
        g32 = g_ref[rows, :].astype(jnp.float32)
        grad_sq = grad_sq + jnp.sum(g32 * g32, axis=0, keepdims=True)
    scale = jnp.sqrt(jnp.full((1, order), jnp.sum(grad_sq), jnp.float32)) / jnp.sqrt(
        jnp.full((1, order), jnp.sum(raw_sq) + EPSILON, jnp.float32)
    )
    for i in range(0, order, NB):
        d = (stat_ref[0, pl.ds(i, NB), :] * scale).reshape(NB // 8, 8, order)
        dir_ref[pl.ds(i // 8, NB // 8)] = d.astype(jnp.bfloat16)


def kernel(
    part_ref, stats_hbm, roots_hbm, owner_hbm, refresh_hbm, out_ref,
    own, pair, recvx, summed, outgoing, gath, ret, dirs, slot_ref, owner_ref, refresh_ref,
    g_ref, gt_ref, stat_ref, root_ref, m0, m1, f0, f1, x0, x1, q0, q1, t0, t1, raw_ref,
    load_sem, own_sem, pair_send, pair_recv, x_send, x_recv, a_send, a_recv, r_send, r_recv, row_sem,
):
    chips, blocks, rows8, order = own.shape
    workers = gath.shape[0]
    g, w = lax.axis_index("dp"), lax.axis_index("worker")
    x, c = lax.div(g, 2), lax.rem(g, 2)
    nc = len(CHUNKS)

    def other_worker(i):
        return lax.rem(w + i, workers)

    barrier = pltpu.get_barrier_semaphore()
    pl.semaphore_signal(barrier, inc=1, device_id=(x * 2 + 1 - c, w), device_id_type=MESH)
    for i in range(1, chips):
        to = lax.rem(x + i, chips) * 2 + c
        pl.semaphore_signal(barrier, inc=1, device_id=(to, w), device_id_type=MESH)

    side = SIDE
    z, y = lax.div(w, side), lax.rem(w, side)
    for i in range(1, side):
        beside = z * side + lax.rem(y + i, side)
        above = lax.rem(z + i, side) * side + y
        pl.semaphore_signal(barrier, inc=1, device_id=(g, beside), device_id_type=MESH)
        pl.semaphore_signal(barrier, inc=1, device_id=(g, above), device_id_type=MESH)

    def own_copy(j, t):
        cols = pl.ds(*CHUNKS[j])
        return pltpu.make_async_copy(
            part_ref.at[t, c, :, :, cols], own.at[t, :, :, cols], own_sem.at[j, t]
        )

    def pair_copy(j, t):
        cols = pl.ds(*CHUNKS[j])
        return pltpu.make_async_remote_copy(
            part_ref.at[t, 1 - c, :, :, cols], pair.at[t, :, :, cols],
            pair_send.at[j, t], pair_recv.at[j, t],
            device_id=(x * 2 + 1 - c, w), device_id_type=MESH,
        )

    def x_copy(j, i):
        cols = pl.ds(*CHUNKS[j])
        to = lax.rem(x + i, chips)
        return pltpu.make_async_remote_copy(
            own.at[to, :, :, cols], recvx.at[i - 1, :, :, cols],
            x_send.at[j, i - 1], x_recv.at[j, i - 1],
            device_id=(to * 2 + c, w), device_id_type=MESH,
        )

    def a_copy(j, to):
        cols = pl.ds(*CHUNKS[j])
        return pltpu.make_async_remote_copy(
            outgoing.at[to, :, cols], gath.at[w, :, cols], a_send.at[j], a_recv.at[j],
            device_id=(g, to), device_id_type=MESH,
        )

    def a_all(j):
        cols, rest = pl.ds(*CHUNKS[j]), pl.ds(0, workers - 1)
        return pltpu.make_async_remote_copy(
            outgoing.at[rest, :, cols], gath.at[rest, :, cols], a_send.at[j], a_recv.at[j],
            device_id=(g, w), device_id_type=MESH,
        )

    def r_copy(to):
        return pltpu.make_async_remote_copy(
            dirs.at[to], ret.at[w], r_send, r_recv, device_id=(g, to), device_id_type=MESH
        )

    def r_all():
        rest = pl.ds(0, workers - 1)
        return pltpu.make_async_remote_copy(
            dirs.at[rest], ret.at[rest], r_send, r_recv, device_id=(g, w), device_id_type=MESH
        )

    hops = (2, 1, 3, 0)
    owner_load = pltpu.make_async_copy(owner_hbm, owner_ref, load_sem.at[2])
    refresh_load = pltpu.make_async_copy(refresh_hbm, refresh_ref, load_sem.at[3])
    owner_load.start()
    refresh_load.start()
    for j in range(nc):
        for i in hops:
            own_copy(j, lax.rem(x + i, chips)).start()
    stat_load = pltpu.make_async_copy(stats_hbm, stat_ref, load_sem.at[0])
    root_load = pltpu.make_async_copy(roots_hbm, root_ref, load_sem.at[1])
    stat_load.start()
    root_load.start()
    pl.semaphore_wait(barrier, chips + 2 * (side - 1))
    for j in range(nc):
        for i in hops:
            pair_copy(j, lax.rem(x + i, chips)).start()
    for i in range(1, side):
        above = lax.rem(z + i, side) * side + y
        pl.semaphore_signal(row_sem.at[z], inc=1, device_id=(g, above), device_id_type=MESH)

    step = 8
    first = g * blocks

    def add_pair(j):
        cols = pl.ds(*CHUNKS[j])
        for i in hops:
            t = lax.rem(x + i, chips)
            own_copy(j, t).wait()
            pair_copy(j, t).wait_recv()
            if i == 0:
                continue
            for k in range(0, blocks, step):
                ks = pl.ds(k, step)
                own[t, ks, :, cols] = (
                    own[t, ks, :, cols].astype(jnp.float32) + pair[t, ks, :, cols].astype(jnp.float32)
                ).astype(jnp.bfloat16)
            x_copy(j, i).start()

    def find_slots():
        owners = [owner_ref[first + k] for k in range(blocks)]

        def find(t, carry):
            slot = jnp.int32(0)
            for k in range(blocks):
                slot = jnp.where(owners[k] == t, k, slot)
            slot_ref[t] = slot
            return carry

        lax.fori_loop(0, workers, find, 0, unroll=2)

    add_pair(0)
    add_pair(1)
    owner_load.wait()
    refresh_load.wait()
    find_slots()
    for j in range(2, nc):
        add_pair(j)

    for j in range(nc):
        cols = pl.ds(*CHUNKS[j])
        for i in range(1, chips):
            x_copy(j, i).wait_recv()
        for k in range(0, blocks, step):
            ks = pl.ds(k, step)
            total = own[x, ks, :, cols].astype(jnp.float32) + pair[x, ks, :, cols].astype(jnp.float32)
            for i in range(chips - 1):
                total = total + recvx[i, ks, :, cols].astype(jnp.float32)
            summed[ks, :, cols] = total.astype(jnp.bfloat16)

        def send(row, i):
            to = row * side + lax.rem(y + i, side)
            outgoing[to, :, cols] = summed[slot_ref[to], :, cols]
            a_copy(j, to).start()

        def send_own_row(i, carry):
            send(z, i)
            return carry

        def send_row(k, carry):
            row = lax.rem(z + k, side)
            if j == 0:
                pl.semaphore_wait(row_sem.at[row], 1)
            lax.fori_loop(0, side, lambda i, c: (send(row, i), c)[1], 0)
            return carry

        lax.fori_loop(1, side, send_own_row, 0)
        lax.fori_loop(1, side, send_row, 0)
        gath[w, :, cols] = summed[slot_ref[w], :, cols]

    mine = first + slot_ref[w]

    def is_listed(i, carry):
        return carry + jnp.where(refresh_ref[i] == mine, 1, 0)

    fresh = lax.fori_loop(0, refresh_ref.shape[0], is_listed, jnp.int32(0))

    for j in range(nc):
        cols = pl.ds(*CHUNKS[j])
        a_all(j).wait_recv()
        for i in range(0, workers, 16):
            piece = gath[pl.ds(i, 16), :, cols].astype(jnp.float32).reshape(16 * rows8, CHUNKS[j][1])
            g_ref[pl.ds(i * rows8, 16 * rows8), cols] = piece.astype(jnp.bfloat16)
        gt_ref[cols, :] = g_ref[:, cols].T
    stat_load.wait()
    root_load.wait()
    take = jnp.full((1, order), fresh, jnp.int32) > 0
    compute(
        take, g_ref, gt_ref, stat_ref, root_ref, (m0, m1), (f0, f1), (x0, x1), (q0, q1), (t0, t1),
        raw_ref, dirs,
    )

    turn = 1 - 2 * lax.rem(z + y, 2)

    def send_back(row):
        def one(i, carry):
            r_copy(row * side + lax.rem(y + turn * i + side, side)).start()
            return carry

        lax.fori_loop(jnp.where(row == z, 1, 0), side, one, 0)

    for half, k in BACK:
        send_back(4 * half + lax.rem(z + k, 4))
    ret[w] = dirs[w]
    for j in range(nc):
        for i in range(chips):
            pair_copy(j, i).wait_send()
        for i in range(1, chips):
            x_copy(j, i).wait_send()
        a_all(j).wait_send()
    r_all().wait_recv()
    for k in range(blocks):
        out_ref[k] = ret[owner_ref[first + k]]
    r_all().wait_send()


def on_device(partials, stats, roots, owner, refresh):
    workers, replicas = lax.axis_size("worker"), lax.axis_size("dp")
    _, total, rows, order = partials.shape
    chips, blocks = replicas // 2, total // replicas
    nc = len(CHUNKS)
    bf, dma = functools.partial(pltpu.VMEM, dtype=jnp.bfloat16), pltpu.SemaphoreType.DMA
    square = bf((order, order))
    return pl.pallas_call(
        kernel,
        out_shape=jax.ShapeDtypeStruct((blocks, rows, order), jnp.bfloat16),
        in_specs=[pl.BlockSpec(memory_space=pltpu.HBM)] * 5,
        out_specs=pl.BlockSpec(memory_space=pltpu.VMEM),
        scratch_shapes=[
            bf((chips, blocks, rows, order)),
            bf((chips, blocks, rows, order)),
            bf((chips - 1, blocks, rows, order)),
            bf((blocks, rows, order)),
            bf((workers, rows, order)),
            bf((workers, rows, order)),
            bf((workers, rows, order)),
            bf((workers, rows, order)),
            pltpu.SMEM((workers,), jnp.int32),
            pltpu.SMEM(owner.shape, jnp.int32),
            pltpu.SMEM(refresh.shape, jnp.int32),
            square,
            square,
            pltpu.VMEM((2, order, order), jnp.float32),
            bf((2, order, order)),
        ]
        + [square] * 10
        + [
            bf((2, order, order)),
            dma((4,)),
            dma((nc, chips)),
            dma((nc, chips)),
            dma((nc, chips)),
            dma((nc, chips - 1)),
            dma((nc, chips - 1)),
            dma((nc,)),
            dma((nc,)),
            dma,
            dma,
            pltpu.SemaphoreType.REGULAR((SIDE,)),
        ],
        compiler_params=pltpu.CompilerParams(
            collective_id=0, has_side_effects=True, vmem_limit_bytes=53 * 2**20 + 2**19
        ),
    )(
        partials.reshape(chips, 2, blocks, rows, order),
        stats.reshape(2, order, order),
        roots.reshape(2, order, order),
        owner,
        refresh,
    )


def solution(mesh):
    in_specs = (
        P("dp", None, "worker", None),
        P("dp", "worker", None, None, None),
        P("dp", "worker", None, None, None),
        P(),
        P(),
    )
    return jax.shard_map(
        on_device,
        mesh=mesh,
        in_specs=in_specs,
        out_specs=P("dp", "worker", None),
        check_vma=False,
    )
```

```python
import functools

import jax
import jax.numpy as jnp
from jax import lax
from jax.experimental import pallas as pl
from jax.experimental.pallas import tpu as pltpu
from jax.sharding import PartitionSpec as P

ITERS = 3
STAT_DECAY = 0.9
EPSILON = 1e-06
MESH = pl.DeviceIdType.MESH
SIDE = 8
BACK = ((0, 0), (0, 1), (1, 0), (0, 2), (0, 3), (1, 1), (1, 2), (1, 3))
CHUNKS = ((0, 128), (128, 128), (256, 256))
NB = 512


def dot(a, b):
    return jnp.dot(a, b, preferred_element_type=jnp.float32)


def dot_nt(a, b):
    return lax.dot_general(a, b, (((1,), (1,)), ((), ())), preferred_element_type=jnp.float32)


def row_blocks(order):
    return [pl.ds(i, NB) for i in range(0, order, NB)]


def product(a_ref, b_ref, c_ref):
    for rows in row_blocks(a_ref.shape[0]):
        c_ref[rows, :] = dot(a_ref[rows, :], b_ref[...]).astype(c_ref.dtype)


def put(rows, m32, m_ref, f_ref):
    shape = m32.shape
    m = m32.astype(jnp.bfloat16)
    row = lax.broadcasted_iota(jnp.int32, shape, 0) + rows.start
    col = lax.broadcasted_iota(jnp.int32, shape, 1)
    five = jnp.where(row == col, 5.0, 0.0)
    m_ref[rows, :] = m
    f_ref[rows, :] = ((five - m.astype(jnp.float32)) * 0.25).astype(jnp.bfloat16)


def normalized(stat_ref, side, left, right, m_ref, f_ref):
    order = m_ref.shape[0]
    total = jnp.zeros((1, order), jnp.float32)
    for rows in row_blocks(order):
        mixed = STAT_DECAY * stat_ref[side, rows, :] + (1.0 - STAT_DECAY) * dot(left[rows, :], right[...])
        stat_ref[side, rows, :] = mixed
        total = total + jnp.sum(mixed * mixed, axis=0, keepdims=True)
    scale = lax.rsqrt(jnp.full((1, order), jnp.sum(total) + EPSILON, jnp.float32))
    for rows in row_blocks(order):
        put(rows, stat_ref[side, rows, :] * scale, m_ref, f_ref)


def compute(take, g_ref, gt_ref, stat_ref, root_ref, m, f, x, q, t, raw_ref, dir_ref):
    order = g_ref.shape[0]
    normalized(stat_ref, 0, g_ref, gt_ref, m[0], f[0])
    normalized(stat_ref, 1, gt_ref, g_ref, m[1], f[1])
    held = [f[0], f[1]]
    factor = [f[0], f[1]]
    spare = [[x[0], t[0]], [x[1], t[1]]]
    for it in range(ITERS - 1):
        if it > 0:
            for s in range(2):
                new = spare[s].pop(0)
                product(held[s], factor[s], new)
                spare[s].append(held[s])
                held[s] = new
        y = [spare[s][0] for s in range(2)]
        for s in range(2):
            product(factor[s], factor[s], q[s])
        for s in range(2):
            product(q[s], m[s], y[s])
        later = [raw_ref.at[s] for s in range(2)] if it == 0 else factor
        for s in range(2):
            for rows in row_blocks(order):
                put(rows, dot(y[s][rows, :], q[s][...]), m[s], later[s])
        factor = later
    for s in range(2):
        new = spare[s].pop(0)
        for rows in row_blocks(order):
            root = dot(held[s][rows, :], factor[s][...])
            old = root_ref[s, rows, :].astype(jnp.float32)
            new[rows, :] = jnp.where(take, root, old).astype(jnp.bfloat16)
        spare[s].append(held[s])
        held[s] = new
    product(held[0], g_ref, q[0])
    grad_sq = jnp.zeros((1, order), jnp.float32)
    raw_sq = jnp.zeros((1, order), jnp.float32)
    for rows in row_blocks(order):
        raw = dot(q[0][rows, :], held[1][...])
        stat_ref[0, rows, :] = raw
        raw_sq = raw_sq + jnp.sum(raw * raw, axis=0, keepdims=True)
        g32 = g_ref[rows, :].astype(jnp.float32)
        grad_sq = grad_sq + jnp.sum(g32 * g32, axis=0, keepdims=True)
    scale = jnp.sqrt(jnp.full((1, order), jnp.sum(grad_sq), jnp.float32)) / jnp.sqrt(
        jnp.full((1, order), jnp.sum(raw_sq) + EPSILON, jnp.float32)
    )
    for i in range(0, order, NB):
        d = (stat_ref[0, pl.ds(i, NB), :] * scale).reshape(NB // 8, 8, order)
        dir_ref[pl.ds(i // 8, NB // 8)] = d.astype(jnp.bfloat16)


def kernel(
    part_ref, stats_hbm, roots_hbm, owner_hbm, refresh_hbm, out_ref,
    own, pair, recvx, summed, outgoing, gath, ret, dirs, slot_ref, owner_ref, refresh_ref,
    g_ref, gt_ref, stat_ref, root_ref, m0, m1, f0, f1, x0, x1, q0, q1, t0, t1, raw_ref,
    load_sem, own_sem, pair_send, pair_recv, x_send, x_recv, a_send, a_recv, r_send, r_recv, row_sem,
):
    chips, blocks, rows8, order = own.shape
    workers = gath.shape[0]
    g, w = lax.axis_index("dp"), lax.axis_index("worker")
    x, c = lax.div(g, 2), lax.rem(g, 2)
    nc = len(CHUNKS)

    def other_worker(i):
        return lax.rem(w + i, workers)

    barrier = pltpu.get_barrier_semaphore()
    pl.semaphore_signal(barrier, inc=1, device_id=(x * 2 + 1 - c, w), device_id_type=MESH)
    for i in range(1, chips):
        to = lax.rem(x + i, chips) * 2 + c
        pl.semaphore_signal(barrier, inc=1, device_id=(to, w), device_id_type=MESH)

    side = SIDE
    z, y = lax.div(w, side), lax.rem(w, side)
    for i in range(1, side):
        beside = z * side + lax.rem(y + i, side)
        above = lax.rem(z + i, side) * side + y
        pl.semaphore_signal(barrier, inc=1, device_id=(g, beside), device_id_type=MESH)
        pl.semaphore_signal(barrier, inc=1, device_id=(g, above), device_id_type=MESH)

    def own_copy(j):
        cols = pl.ds(*CHUNKS[j])
        return pltpu.make_async_copy(
            part_ref.at[:, c, :, :, cols], own.at[:, :, :, cols], own_sem.at[j]
        )

    def pair_copy(j, t):
        cols = pl.ds(*CHUNKS[j])
        return pltpu.make_async_remote_copy(
            part_ref.at[t, 1 - c, :, :, cols], pair.at[t, :, :, cols],
            pair_send.at[j, t], pair_recv.at[j, t],
            device_id=(x * 2 + 1 - c, w), device_id_type=MESH,
        )

    def x_copy(j, i):
        cols = pl.ds(*CHUNKS[j])
        to = lax.rem(x + i, chips)
        return pltpu.make_async_remote_copy(
            own.at[to, :, :, cols], recvx.at[i - 1, :, :, cols],
            x_send.at[j, i - 1], x_recv.at[j, i - 1],
            device_id=(to * 2 + c, w), device_id_type=MESH,
        )

    def a_copy(j, to):
        cols = pl.ds(*CHUNKS[j])
        return pltpu.make_async_remote_copy(
            outgoing.at[to, :, cols], gath.at[w, :, cols], a_send.at[j], a_recv.at[j],
            device_id=(g, to), device_id_type=MESH,
        )

    def a_all(j):
        cols, rest = pl.ds(*CHUNKS[j]), pl.ds(0, workers - 1)
        return pltpu.make_async_remote_copy(
            outgoing.at[rest, :, cols], gath.at[rest, :, cols], a_send.at[j], a_recv.at[j],
            device_id=(g, w), device_id_type=MESH,
        )

    def r_copy(to):
        return pltpu.make_async_remote_copy(
            dirs.at[to], ret.at[w], r_send, r_recv, device_id=(g, to), device_id_type=MESH
        )

    def r_all():
        rest = pl.ds(0, workers - 1)
        return pltpu.make_async_remote_copy(
            dirs.at[rest], ret.at[rest], r_send, r_recv, device_id=(g, w), device_id_type=MESH
        )

    hops = (2, 1, 3, 0)
    own_copy(0).start()
    pl.semaphore_wait(barrier, chips + 2 * (side - 1))
    for j in range(nc):
        for i in hops:
            pair_copy(j, lax.rem(x + i, chips)).start()
        if j > 0:
            own_copy(j).start()
    owner_load = pltpu.make_async_copy(owner_hbm, owner_ref, load_sem.at[2])
    refresh_load = pltpu.make_async_copy(refresh_hbm, refresh_ref, load_sem.at[3])
    owner_load.start()
    refresh_load.start()
    for i in range(1, side):
        above = lax.rem(z + i, side) * side + y
        pl.semaphore_signal(row_sem.at[z], inc=1, device_id=(g, above), device_id_type=MESH)

    step = 8
    first = g * blocks

    def add_pair(j):
        cols = pl.ds(*CHUNKS[j])
        own_copy(j).wait()
        for i in hops:
            t = lax.rem(x + i, chips)
            pair_copy(j, t).wait_recv()
            if i == 0:
                continue
            for k in range(0, blocks, step):
                ks = pl.ds(k, step)
                own[t, ks, :, cols] = (
                    own[t, ks, :, cols].astype(jnp.float32) + pair[t, ks, :, cols].astype(jnp.float32)
                ).astype(jnp.bfloat16)
            x_copy(j, i).start()

    def find_slots():
        owners = [owner_ref[first + k] for k in range(blocks)]

        def find(t, carry):
            slot = jnp.int32(0)
            for k in range(blocks):
                slot = jnp.where(owners[k] == t, k, slot)
            slot_ref[t] = slot
            return carry

        lax.fori_loop(0, workers, find, 0, unroll=2)

    add_pair(0)
    add_pair(1)
    owner_load.wait()
    refresh_load.wait()
    find_slots()
    for j in range(2, nc):
        add_pair(j)
    stat_load = pltpu.make_async_copy(stats_hbm, stat_ref, load_sem.at[0])
    root_load = pltpu.make_async_copy(roots_hbm, root_ref, load_sem.at[1])
    stat_load.start()
    root_load.start()

    for j in range(nc):
        cols = pl.ds(*CHUNKS[j])
        for i in range(1, chips):
            x_copy(j, i).wait_recv()
        for k in range(0, blocks, step):
            ks = pl.ds(k, step)
            total = own[x, ks, :, cols].astype(jnp.float32) + pair[x, ks, :, cols].astype(jnp.float32)
            for i in range(chips - 1):
                total = total + recvx[i, ks, :, cols].astype(jnp.float32)
            summed[ks, :, cols] = total.astype(jnp.bfloat16)

        def send(row, i):
            to = row * side + lax.rem(y + i, side)
            outgoing[to, :, cols] = summed[slot_ref[to], :, cols]
            a_copy(j, to).start()

        def send_own_row(i, carry):
            send(z, i)
            return carry

        def send_row(k, carry):
            row = lax.rem(z + k, side)
            if j == 0:
                pl.semaphore_wait(row_sem.at[row], 1)
            lax.fori_loop(0, side, lambda i, c: (send(row, i), c)[1], 0)
            return carry

        lax.fori_loop(1, side, send_own_row, 0)
        lax.fori_loop(1, side, send_row, 0)
        gath[w, :, cols] = summed[slot_ref[w], :, cols]

    mine = first + slot_ref[w]

    def is_listed(i, carry):
        return carry + jnp.where(refresh_ref[i] == mine, 1, 0)

    fresh = lax.fori_loop(0, refresh_ref.shape[0], is_listed, jnp.int32(0))

    for j in range(nc):
        cols = pl.ds(*CHUNKS[j])
        a_all(j).wait_recv()
        for i in range(0, workers, 16):
            piece = gath[pl.ds(i, 16), :, cols].astype(jnp.float32).reshape(16 * rows8, CHUNKS[j][1])
            g_ref[pl.ds(i * rows8, 16 * rows8), cols] = piece.astype(jnp.bfloat16)
        gt_ref[cols, :] = g_ref[:, cols].T
    stat_load.wait()
    root_load.wait()
    take = jnp.full((1, order), fresh, jnp.int32) > 0
    compute(
        take, g_ref, gt_ref, stat_ref, root_ref, (m0, m1), (f0, f1), (x0, x1), (q0, q1), (t0, t1),
        raw_ref, dirs,
    )

    turn = 1 - 2 * lax.rem(z + y, 2)

    def send_back(row):
        def one(i, carry):
            r_copy(row * side + lax.rem(y + turn * i + side, side)).start()
            return carry

        lax.fori_loop(jnp.where(row == z, 1, 0), side, one, 0)

    for half, k in BACK:
        send_back(4 * half + lax.rem(z + k, 4))
    ret[w] = dirs[w]
    for j in range(nc):
        for i in range(chips):
            pair_copy(j, i).wait_send()
        for i in range(1, chips):
            x_copy(j, i).wait_send()
        a_all(j).wait_send()
    r_all().wait_recv()
    for k in range(blocks):
        out_ref[k] = ret[owner_ref[first + k]]
    r_all().wait_send()


def on_device(partials, stats, roots, owner, refresh):
    workers, replicas = lax.axis_size("worker"), lax.axis_size("dp")
    _, total, rows, order = partials.shape
    chips, blocks = replicas // 2, total // replicas
    nc = len(CHUNKS)
    bf, dma = functools.partial(pltpu.VMEM, dtype=jnp.bfloat16), pltpu.SemaphoreType.DMA
    square = bf((order, order))
    return pl.pallas_call(
        kernel,
        out_shape=pltpu.VMEM((blocks, rows, order), jnp.bfloat16),
        in_specs=[pl.BlockSpec(memory_space=pltpu.HBM)] * 5,
        out_specs=pl.BlockSpec(memory_space=pltpu.VMEM),
        scratch_shapes=[
            bf((chips, blocks, rows, order)),
            bf((chips, blocks, rows, order)),
            bf((chips - 1, blocks, rows, order)),
            bf((blocks, rows, order)),
            bf((workers, rows, order)),
            bf((workers, rows, order)),
            bf((workers, rows, order)),
            bf((workers, rows, order)),
            pltpu.SMEM((workers,), jnp.int32),
            pltpu.SMEM(owner.shape, jnp.int32),
            pltpu.SMEM(refresh.shape, jnp.int32),
            square,
            square,
            pltpu.VMEM((2, order, order), jnp.float32),
            bf((2, order, order)),
        ]
        + [square] * 10
        + [
            bf((2, order, order)),
            dma((4,)),
            dma((nc,)),
            dma((nc, chips)),
            dma((nc, chips)),
            dma((nc, chips - 1)),
            dma((nc, chips - 1)),
            dma((nc,)),
            dma((nc,)),
            dma,
            dma,
            pltpu.SemaphoreType.REGULAR((SIDE,)),
        ],
        compiler_params=pltpu.CompilerParams(
            collective_id=0, has_side_effects=True, vmem_limit_bytes=56 * 2**20
        ),
    )(
        partials.reshape(chips, 2, blocks, rows, order),
        stats.reshape(2, order, order),
        roots.reshape(2, order, order),
        owner,
        refresh,
    )


def solution(mesh):
    in_specs = (
        P("dp", None, "worker", None),
        P("dp", "worker", None, None, None),
        P("dp", "worker", None, None, None),
        P(),
        P(),
    )
    return jax.shard_map(
        on_device,
        mesh=mesh,
        in_specs=in_specs,
        out_specs=P("dp", "worker", None),
        check_vma=False,
    )
```

```python
import functools

import jax
import jax.numpy as jnp
from jax import lax
from jax.experimental import pallas as pl
from jax.experimental.pallas import tpu as pltpu
from jax.sharding import PartitionSpec as P

ITERS = 3
STAT_DECAY = 0.9
EPSILON = 1e-06
MESH = pl.DeviceIdType.MESH
SIDE = 8
BACK = ((0, 0), (0, 1), (1, 0), (0, 2), (0, 3), (1, 1), (1, 2), (1, 3))
CHUNKS = ((0, 128), (128, 128), (256, 256))
NB = 512


def dot(a, b):
    return jnp.dot(a, b, preferred_element_type=jnp.float32)


def dot_nt(a, b):
    return lax.dot_general(a, b, (((1,), (1,)), ((), ())), preferred_element_type=jnp.float32)


def row_blocks(order):
    return [pl.ds(i, NB) for i in range(0, order, NB)]


def product(a_ref, b_ref, c_ref):
    for rows in row_blocks(a_ref.shape[0]):
        c_ref[rows, :] = dot(a_ref[rows, :], b_ref[...]).astype(c_ref.dtype)


def put(rows, m32, m_ref, f_ref):
    shape = m32.shape
    m = m32.astype(jnp.bfloat16)
    row = lax.broadcasted_iota(jnp.int32, shape, 0) + rows.start
    col = lax.broadcasted_iota(jnp.int32, shape, 1)
    five = jnp.where(row == col, 5.0, 0.0)
    m_ref[rows, :] = m
    f_ref[rows, :] = ((five - m.astype(jnp.float32)) * 0.25).astype(jnp.bfloat16)


def normalized(stat_ref, side, left, right, m_ref, f_ref):
    order = m_ref.shape[0]
    total = jnp.zeros((1, order), jnp.float32)
    for rows in row_blocks(order):
        mixed = STAT_DECAY * stat_ref[side, rows, :] + (1.0 - STAT_DECAY) * dot(left[rows, :], right[...])
        stat_ref[side, rows, :] = mixed
        total = total + jnp.sum(mixed * mixed, axis=0, keepdims=True)
    scale = lax.rsqrt(jnp.full((1, order), jnp.sum(total) + EPSILON, jnp.float32))
    for rows in row_blocks(order):
        put(rows, stat_ref[side, rows, :] * scale, m_ref, f_ref)


def compute(take, g_ref, gt_ref, stat_ref, root_ref, m, f, x, q, t, raw_ref):
    order = g_ref.shape[0]
    normalized(stat_ref, 0, g_ref, gt_ref, m[0], f[0])
    normalized(stat_ref, 1, gt_ref, g_ref, m[1], f[1])
    held = [f[0], f[1]]
    factor = [f[0], f[1]]
    spare = [[x[0], t[0]], [x[1], t[1]]]
    for it in range(ITERS - 1):
        if it > 0:
            for s in range(2):
                new = spare[s].pop(0)
                product(held[s], factor[s], new)
                spare[s].append(held[s])
                held[s] = new
        y = [spare[s][0] for s in range(2)]
        for s in range(2):
            product(factor[s], factor[s], q[s])
        for s in range(2):
            product(q[s], m[s], y[s])
        later = [raw_ref.at[s] for s in range(2)] if it == 0 else factor
        for s in range(2):
            for rows in row_blocks(order):
                put(rows, dot(y[s][rows, :], q[s][...]), m[s], later[s])
        factor = later
    for s in range(2):
        new = spare[s].pop(0)
        for rows in row_blocks(order):
            root = dot(held[s][rows, :], factor[s][...])
            old = root_ref[s, rows, :].astype(jnp.float32)
            new[rows, :] = jnp.where(take, root, old).astype(jnp.bfloat16)
        spare[s].append(held[s])
        held[s] = new
    product(held[0], g_ref, q[0])
    grad_sq = jnp.zeros((1, order), jnp.float32)
    raw_sq = jnp.zeros((1, order), jnp.float32)
    for rows in row_blocks(order):
        raw = dot(q[0][rows, :], held[1][...])
        stat_ref[0, rows, :] = raw
        raw_sq = raw_sq + jnp.sum(raw * raw, axis=0, keepdims=True)
        g32 = g_ref[rows, :].astype(jnp.float32)
        grad_sq = grad_sq + jnp.sum(g32 * g32, axis=0, keepdims=True)
    return jnp.sqrt(jnp.full((1, order), jnp.sum(grad_sq), jnp.float32)) / jnp.sqrt(
        jnp.full((1, order), jnp.sum(raw_sq) + EPSILON, jnp.float32)
    )


def kernel(
    part_ref, stats_hbm, roots_hbm, owner_hbm, refresh_hbm, out_ref,
    own, pair, recvx, summed, outgoing, gath, ret, dirs, slot_ref, owner_ref, refresh_ref,
    g_ref, gt_ref, stat_ref, root_ref, m0, m1, f0, f1, x0, x1, q0, q1, t0, t1, raw_ref,
    load_sem, own_sem, pair_send, pair_recv, x_send, x_recv, a_send, a_recv, r_send, r_recv, row_sem,
):
    chips, blocks, rows8, order = own.shape
    workers = gath.shape[0]
    g, w = lax.axis_index("dp"), lax.axis_index("worker")
    x, c = lax.div(g, 2), lax.rem(g, 2)
    nc = len(CHUNKS)

    def other_worker(i):
        return lax.rem(w + i, workers)

    barrier = pltpu.get_barrier_semaphore()
    pl.semaphore_signal(barrier, inc=1, device_id=(x * 2 + 1 - c, w), device_id_type=MESH)
    for i in range(1, chips):
        to = lax.rem(x + i, chips) * 2 + c
        pl.semaphore_signal(barrier, inc=1, device_id=(to, w), device_id_type=MESH)

    side = SIDE
    z, y = lax.div(w, side), lax.rem(w, side)
    for i in range(1, side):
        beside = z * side + lax.rem(y + i, side)
        above = lax.rem(z + i, side) * side + y
        pl.semaphore_signal(barrier, inc=1, device_id=(g, beside), device_id_type=MESH)
        pl.semaphore_signal(barrier, inc=1, device_id=(g, above), device_id_type=MESH)

    def own_copy(j):
        cols = pl.ds(*CHUNKS[j])
        return pltpu.make_async_copy(
            part_ref.at[:, c, :, :, cols], own.at[:, :, :, cols], own_sem.at[j]
        )

    def pair_copy(j, t):
        cols = pl.ds(*CHUNKS[j])
        return pltpu.make_async_remote_copy(
            part_ref.at[t, 1 - c, :, :, cols], pair.at[t, :, :, cols],
            pair_send.at[j, t], pair_recv.at[j, t],
            device_id=(x * 2 + 1 - c, w), device_id_type=MESH,
        )

    def x_copy(j, i):
        cols = pl.ds(*CHUNKS[j])
        to = lax.rem(x + i, chips)
        return pltpu.make_async_remote_copy(
            own.at[to, :, :, cols], recvx.at[i - 1, :, :, cols],
            x_send.at[j, i - 1], x_recv.at[j, i - 1],
            device_id=(to * 2 + c, w), device_id_type=MESH,
        )

    def a_copy(j, to):
        cols = pl.ds(*CHUNKS[j])
        return pltpu.make_async_remote_copy(
            outgoing.at[to, :, cols], gath.at[w, :, cols], a_send.at[j], a_recv.at[j],
            device_id=(g, to), device_id_type=MESH,
        )

    def a_all(j):
        cols, rest = pl.ds(*CHUNKS[j]), pl.ds(0, workers - 1)
        return pltpu.make_async_remote_copy(
            outgoing.at[rest, :, cols], gath.at[rest, :, cols], a_send.at[j], a_recv.at[j],
            device_id=(g, w), device_id_type=MESH,
        )

    def r_copy(to):
        return pltpu.make_async_remote_copy(
            dirs.at[to], ret.at[w], r_send, r_recv, device_id=(g, to), device_id_type=MESH
        )

    def r_all():
        rest = pl.ds(0, workers - 1)
        return pltpu.make_async_remote_copy(
            dirs.at[rest], ret.at[rest], r_send, r_recv, device_id=(g, w), device_id_type=MESH
        )

    hops = (2, 1, 3, 0)
    own_copy(0).start()
    pl.semaphore_wait(barrier, chips + 2 * (side - 1))
    for j in range(nc):
        for i in hops:
            pair_copy(j, lax.rem(x + i, chips)).start()
        if j > 0:
            own_copy(j).start()
    owner_load = pltpu.make_async_copy(owner_hbm, owner_ref, load_sem.at[2])
    refresh_load = pltpu.make_async_copy(refresh_hbm, refresh_ref, load_sem.at[3])
    owner_load.start()
    refresh_load.start()
    for i in range(1, side):
        above = lax.rem(z + i, side) * side + y
        pl.semaphore_signal(row_sem.at[z], inc=1, device_id=(g, above), device_id_type=MESH)

    step = 8
    first = g * blocks

    def add_pair(j):
        cols = pl.ds(*CHUNKS[j])
        own_copy(j).wait()
        for i in hops:
            t = lax.rem(x + i, chips)
            pair_copy(j, t).wait_recv()
            if i == 0:
                continue
            for k in range(0, blocks, step):
                ks = pl.ds(k, step)
                own[t, ks, :, cols] = (
                    own[t, ks, :, cols].astype(jnp.float32) + pair[t, ks, :, cols].astype(jnp.float32)
                ).astype(jnp.bfloat16)
            x_copy(j, i).start()

    def find_slots():
        owners = [owner_ref[first + k] for k in range(blocks)]

        def find(t, carry):
            slot = jnp.int32(0)
            for k in range(blocks):
                slot = jnp.where(owners[k] == t, k, slot)
            slot_ref[t] = slot
            return carry

        lax.fori_loop(0, workers, find, 0, unroll=2)

    add_pair(0)
    add_pair(1)
    owner_load.wait()
    refresh_load.wait()
    find_slots()
    for j in range(2, nc):
        add_pair(j)
    stat_load = pltpu.make_async_copy(stats_hbm, stat_ref, load_sem.at[0])
    root_load = pltpu.make_async_copy(roots_hbm, root_ref, load_sem.at[1])
    stat_load.start()
    root_load.start()

    for j in range(nc):
        cols = pl.ds(*CHUNKS[j])
        for i in range(1, chips):
            x_copy(j, i).wait_recv()
        for k in range(0, blocks, step):
            ks = pl.ds(k, step)
            total = own[x, ks, :, cols].astype(jnp.float32) + pair[x, ks, :, cols].astype(jnp.float32)
            for i in range(chips - 1):
                total = total + recvx[i, ks, :, cols].astype(jnp.float32)
            summed[ks, :, cols] = total.astype(jnp.bfloat16)

        def send(row, i):
            to = row * side + lax.rem(y + i, side)
            outgoing[to, :, cols] = summed[slot_ref[to], :, cols]
            a_copy(j, to).start()

        def send_own_row(i, carry):
            send(z, i)
            return carry

        def send_row(k, carry):
            row = lax.rem(z + k, side)
            if j == 0:
                pl.semaphore_wait(row_sem.at[row], 1)
            lax.fori_loop(0, side, lambda i, c: (send(row, i), c)[1], 0)
            return carry

        lax.fori_loop(1, side, send_own_row, 0)
        lax.fori_loop(1, side, send_row, 0)
        gath[w, :, cols] = summed[slot_ref[w], :, cols]

    mine = first + slot_ref[w]

    def is_listed(i, carry):
        return carry + jnp.where(refresh_ref[i] == mine, 1, 0)

    fresh = lax.fori_loop(0, refresh_ref.shape[0], is_listed, jnp.int32(0))

    for j in range(nc):
        cols = pl.ds(*CHUNKS[j])
        a_all(j).wait_recv()
        for i in range(0, workers, 16):
            piece = gath[pl.ds(i, 16), :, cols].astype(jnp.float32).reshape(16 * rows8, CHUNKS[j][1])
            g_ref[pl.ds(i * rows8, 16 * rows8), cols] = piece.astype(jnp.bfloat16)
        gt_ref[cols, :] = g_ref[:, cols].T
    stat_load.wait()
    root_load.wait()
    take = jnp.full((1, order), fresh, jnp.int32) > 0
    scale = compute(
        take, g_ref, gt_ref, stat_ref, root_ref, (m0, m1), (f0, f1), (x0, x1), (q0, q1), (t0, t1),
        raw_ref,
    )

    turn = 1 - 2 * lax.rem(z + y, 2)

    def send_back(row):
        high = side * rows8
        raw = stat_ref[0, pl.ds(pl.multiple_of(row * high, high), high), :]
        dirs[pl.ds(row * side, side)] = (raw * scale).reshape(side, rows8, order).astype(jnp.bfloat16)

        def one(i, carry):
            r_copy(row * side + lax.rem(y + turn * i + side, side)).start()
            return carry

        lax.fori_loop(jnp.where(row == z, 1, 0), side, one, 0)

    for half, k in BACK:
        send_back(4 * half + lax.rem(z + k, 4))
    ret[w] = dirs[w]
    for j in range(nc):
        for i in range(chips):
            pair_copy(j, i).wait_send()
        for i in range(1, chips):
            x_copy(j, i).wait_send()
        a_all(j).wait_send()
    r_all().wait_recv()
    for k in range(blocks):
        out_ref[k] = ret[owner_ref[first + k]]
    r_all().wait_send()


def on_device(partials, stats, roots, owner, refresh):
    workers, replicas = lax.axis_size("worker"), lax.axis_size("dp")
    _, total, rows, order = partials.shape
    chips, blocks = replicas // 2, total // replicas
    nc = len(CHUNKS)
    bf, dma = functools.partial(pltpu.VMEM, dtype=jnp.bfloat16), pltpu.SemaphoreType.DMA
    square = bf((order, order))
    return pl.pallas_call(
        kernel,
        out_shape=pltpu.VMEM((blocks, rows, order), jnp.bfloat16),
        in_specs=[pl.BlockSpec(memory_space=pltpu.HBM)] * 5,
        out_specs=pl.BlockSpec(memory_space=pltpu.VMEM),
        scratch_shapes=[
            bf((chips, blocks, rows, order)),
            bf((chips, blocks, rows, order)),
            bf((chips - 1, blocks, rows, order)),
            bf((blocks, rows, order)),
            bf((workers, rows, order)),
            bf((workers, rows, order)),
            bf((workers, rows, order)),
            bf((workers, rows, order)),
            pltpu.SMEM((workers,), jnp.int32),
            pltpu.SMEM(owner.shape, jnp.int32),
            pltpu.SMEM(refresh.shape, jnp.int32),
            square,
            square,
            pltpu.VMEM((2, order, order), jnp.float32),
            bf((2, order, order)),
        ]
        + [square] * 10
        + [
            bf((2, order, order)),
            dma((4,)),
            dma((nc,)),
            dma((nc, chips)),
            dma((nc, chips)),
            dma((nc, chips - 1)),
            dma((nc, chips - 1)),
            dma((nc,)),
            dma((nc,)),
            dma,
            dma,
            pltpu.SemaphoreType.REGULAR((SIDE,)),
        ],
        compiler_params=pltpu.CompilerParams(
            collective_id=0, has_side_effects=True, vmem_limit_bytes=56 * 2**20
        ),
    )(
        partials.reshape(chips, 2, blocks, rows, order),
        stats.reshape(2, order, order),
        roots.reshape(2, order, order),
        owner,
        refresh,
    )


def solution(mesh):
    in_specs = (
        P("dp", None, "worker", None),
        P("dp", "worker", None, None, None),
        P("dp", "worker", None, None, None),
        P(),
        P(),
    )
    return jax.shard_map(
        on_device,
        mesh=mesh,
        in_specs=in_specs,
        out_specs=P("dp", "worker", None),
        check_vma=False,
    )
```
